128 devices in a mesh: gx: 8 (over x, core), gy: 16 (over y, z).
Axes of the slice: x: 4, y: 4, z: 4, core: 2. Of those that a mesh axis runs over, the one named last changes fastest.
Arguments:
- psi: float32 [2, 2, 160, 320, 128], P(None, None, 'gx', 'gy'), may hold values from -18 to 18
- basis: float32 [2, 8, 160, 320, 128], P(None, None, 'gx', 'gy'), may hold values from -81 to 81
- potential: float32 [160, 320, 128], P('gx', 'gy'), may hold values from -3 to 1
Outputs:
- psi_half: float32 [2, 2, 160, 320, 128], P(None, None, 'gx', 'gy')
The draws below stay inside these ranges and needn't reach their ends.
All inputs are finite; a program needn't handle non-finite values.
Results may differ from the reference program's by a relative error of at most 0.003.
Values sent between devices are 32-bit elements; how exact they have to be, the bound alone decides.
A program may use at most 192 MiB of HBM per device.

```python
import jax
import jax.numpy as jnp
from jax import lax

KCOL = 8
ORBS = 2
NX = 160
NY = 320
NZ = 128


def orbitals(key):
    gauss_key = jax.random.fold_in(key, 11)
    shape = (ORBS, 2, NX, NY, NZ)
    gauss = jax.random.truncated_normal(gauss_key, -6.0, 6.0, shape, jnp.float32)
    base = gauss
    along_x = jnp.arange(NX, dtype=jnp.float32) / NX
    along_y = jnp.arange(NY, dtype=jnp.float32) / NY
    envelope = 0.3 * jnp.exp(jnp.log(10.0) * 0.5 * (along_x[:, None] + along_y[None, :]))
    return (base * envelope[:, :, None], envelope)


def draw_psi(key, part):
    anchor = key
    shared, envelope = orbitals(anchor)
    return shared


def draw_basis(key, part):
    anchor = key
    key = jax.random.fold_in(key, 2)
    shared, envelope = orbitals(anchor)
    mixing = jax.random.uniform(jax.random.fold_in(key, 5), (KCOL, ORBS, 2), jnp.float32, -1.0, 1.0)
    noise = 0.5 * jax.random.truncated_normal(jax.random.fold_in(key, 6), -6.0, 6.0, (2, KCOL, NX, NY, NZ), jnp.float32)
    noise = noise * envelope[None, None, :, :, None]
    real_sum = jnp.zeros((KCOL, NX, NY, NZ), jnp.float32)
    imag_sum = jnp.zeros((KCOL, NX, NY, NZ), jnp.float32)
    for orbit in range(ORBS):
        mix_real = mixing[:, orbit, 0][:, None, None, None]
        mix_imag = mixing[:, orbit, 1][:, None, None, None]
        real_sum = real_sum + mix_real * shared[orbit, 0][None] - mix_imag * shared[orbit, 1][None]
        imag_sum = imag_sum + mix_real * shared[orbit, 1][None] + mix_imag * shared[orbit, 0][None]
    return jnp.stack([real_sum, imag_sum], 0) + noise


def block_levels(own_key, extent, cuts, low, largest):
    level = 1.0
    for dim, shards_of in cuts:
        heights = jax.random.uniform(jax.random.fold_in(jax.random.fold_in(own_key, 6), dim), (shards_of,), jnp.float32, low / len(cuts), largest / len(cuts))
        level = level * jnp.repeat(jnp.exp(heights), extent[dim] // shards_of).reshape((-1,) + (1,) * (len(extent) - 1 - dim))
    return level


def setup_inputs(seed: int = 0) -> dict:
    keys = jax.random.split(jax.random.key(seed), 4)
    psi = draw_psi(jax.random.fold_in(keys[3], 71), 0)
    basis = draw_basis(jax.random.fold_in(keys[3], 71), 0)
    potential = jnp.clip(-3.0 + 4.0 * jax.random.uniform(keys[2], (NX, NY, NZ), jnp.float32) ** block_levels(keys[2], (NX, NY, NZ), ((0, 8), (1, 16)), -0.2, 0.2), -3.0, 1.0)
    return {"psi": psi, "basis": basis, "potential": potential}


coefficients = [-5369.0 / 1800.0, 12.0 / 7.0, -15.0 / 56.0, 10.0 / 189.0, -1.0 / 112.0, 2.0 / 1925.0, -1.0 / 16632.0]
step_size = 0.25


def laplace(padded):
    width_x = padded.shape[2] - 12
    width_y = padded.shape[3] - 12
    center = padded[:, :, 6:6 + width_x, 6:6 + width_y, :]
    total = (3.0 * coefficients[0]) * center
    for offset in range(1, 7):
        near = padded[:, :, 6 + offset:6 + offset + width_x, 6:6 + width_y, :]
        near = near + padded[:, :, 6 - offset:6 - offset + width_x, 6:6 + width_y, :]
        near = near + padded[:, :, 6:6 + width_x, 6 + offset:6 + offset + width_y, :]
        near = near + padded[:, :, 6:6 + width_x, 6 - offset:6 - offset + width_y, :]
        near = near + jnp.roll(center, offset, axis=4) + jnp.roll(center, -offset, axis=4)
        total = total + coefficients[offset] * near
    return total, center


def cross_terms(field, basis):
    flat_field = field.reshape(4, -1)
    flat_basis = basis.reshape(2 * basis.shape[1], -1)
    cross = lax.dot_general(flat_basis, flat_field, (((1,), (1,)), ((), ())), precision=lax.Precision.HIGHEST)
    return cross


def split_intersections(cross, count):
    parts = cross.reshape(2, count, 2, 2)
    real_part = parts[0, :, :, 0] + parts[1, :, :, 1]
    imag_part = parts[0, :, :, 1] - parts[1, :, :, 0]
    return real_part, imag_part


def hamiltonian(padded, potential, basis, real_part, imag_part):
    lap_term, center = laplace(padded)
    kinetic = -0.5 * lap_term + potential[None, None] * center
    high = lax.Precision.HIGHEST
    corr_real = jnp.einsum('kxyz,kj->jxyz', basis[0], real_part, precision=high) - jnp.einsum('kxyz,kj->jxyz', basis[1], imag_part, precision=high)
    corr_imag = jnp.einsum('kxyz,kj->jxyz', basis[0], imag_part, precision=high) + jnp.einsum('kxyz,kj->jxyz', basis[1], real_part, precision=high)
    return jnp.stack([kinetic[:, 0] - corr_real, kinetic[:, 1] - corr_imag], 1)


def advance(applied, term_index):
    factor = step_size / term_index
    return jnp.stack([factor * applied[:, 1], -factor * applied[:, 0]], 1)


def reference(psi, basis, potential):
    ncell = psi.shape[2] * psi.shape[3] * psi.shape[4]
    term = psi
    result = psi
    for term_index in range(1, 5):
        padded = jnp.pad(term, ((0, 0), (0, 0), (6, 6), (6, 6), (0, 0)), mode="wrap")
        cross = cross_terms(term, basis) / ncell
        real_part, imag_part = split_intersections(cross, basis.shape[1])
        applied = hamiltonian(padded, potential, basis, real_part, imag_part)
        term = advance(applied, term_index)
        result = result + term
    return result
```

```python
import functools

import jax
import jax.numpy as jnp
from jax import lax
from jax.experimental import pallas as pl
from jax.experimental.pallas import tpu as pltpu
from jax.sharding import PartitionSpec as P

MESH = pl.DeviceIdType.MESH
coefficients = [
    -5369.0 / 1800.0,
    12.0 / 7.0,
    -15.0 / 56.0,
    10.0 / 189.0,
    -1.0 / 112.0,
    2.0 / 1925.0,
    -1.0 / 16632.0,
]
step_size = 0.25
TERMS = 4
ORBS = 2
KCOL = 8
R = 6


def kernel(sizes, psi_hbm, basis_hbm, pot_hbm, out_hbm, tb, basis, pot, yw, stage, acc, ysend, yrecv, rows, msg, sums,
           load_sem, x_ssem, x_rsem, y_ssem, y_rsem, a_ssem, a_rsem, b_ssem, b_rsem):
    ngx, ngy, ncell = sizes
    width_x, width_y = psi_hbm.shape[2], psi_hbm.shape[3]
    gx, gy = lax.axis_index("gx"), lax.axis_index("gy")
    x_near = [(lax.rem(gx + d, ngx), gy) for d in (ngx - 1, 1)]
    y_near = [(gx, lax.rem(gy + d, ngy)) for d in (ngy - 1, 1)]
    x_peers = [(lax.rem(gx + i, ngx), gy) for i in range(1, ngx)]
    y_peers = [(gx, lax.rem(gy + i, ngy)) for i in range(1, ngy)]

    loads = []
    for j in range(ORBS):
        loads.append(pltpu.make_async_copy(psi_hbm.at[j], tb.at[0, j, :, pl.ds(R, width_x)], load_sem.at[j]))
    loads.append(pltpu.make_async_copy(basis_hbm, basis, load_sem.at[2]))
    loads.append(pltpu.make_async_copy(pot_hbm, pot, load_sem.at[3]))
    for copy in loads:
        copy.start()
    barrier = pltpu.get_barrier_semaphore()
    for peer in x_peers + y_peers:
        pl.semaphore_signal(barrier, inc=1, device_id=peer, device_id_type=MESH)
    rows[...] = jnp.zeros_like(rows)

    pending = []

    def pack(n, j, c, x4, t4):
        base = pl.multiple_of(c * R * width_x + x4 * 4 * R, 8)
        low = ysend.at[n, j, 0, pl.ds(base, 4 * R)]
        high = ysend.at[n, j, 1, pl.ds(base, 4 * R)]
        for i, t in enumerate(t4):
            low[pl.ds(R * i, R), :] = t[0:R]
            high[pl.ds(R * i, R), :] = t[width_y - R:width_y]

    def send(n, j):
        for side in range(2):
            src = R if side == 0 else width_x
            dst = width_x + R if side == 0 else 0
            copy = pltpu.make_async_remote_copy(
                src_ref=ysend.at[n, j, side], dst_ref=yrecv.at[n, j, 1 - side],
                send_sem=y_ssem.at[n, j, side], recv_sem=y_rsem.at[n, j, 1 - side],
                device_id=y_near[side], device_id_type=MESH)
            copy.start()
            pending.append(copy)
            copy = pltpu.make_async_remote_copy(
                src_ref=tb.at[n, j, :, pl.ds(src, R)], dst_ref=tb.at[n, j, :, pl.ds(dst, R)],
                send_sem=x_ssem.at[n, j, side], recv_sem=x_rsem.at[n, j, 1 - side],
                device_id=x_near[side], device_id_type=MESH)
            copy.start()
            pending.append(copy)

    def receive(n, j):
        for side in range(2):
            pltpu.make_async_remote_copy(
                src_ref=ysend.at[n, j, 1 - side], dst_ref=yrecv.at[n, j, side],
                send_sem=y_ssem.at[n, j, 1 - side], recv_sem=y_rsem.at[n, j, side],
                device_id=y_near[side], device_id_type=MESH).wait_recv()
            src = R if side == 1 else width_x
            dst = width_x + R if side == 1 else 0
            pltpu.make_async_remote_copy(
                src_ref=tb.at[n, j, :, pl.ds(src, R)], dst_ref=tb.at[n, j, :, pl.ds(dst, R)],
                send_sem=x_ssem.at[n, j, 1 - side], recv_sem=x_rsem.at[n, j, side],
                device_id=x_near[side], device_id_type=MESH).wait_recv()

        def unpack(x4, carry):
            for c in range(2):
                base = pl.multiple_of(c * R * width_x + x4 * 4 * R, 8)
                low = yrecv.at[n, j, 0, pl.ds(base, 4 * R)]
                high = yrecv.at[n, j, 1, pl.ds(base, 4 * R)]
                for i in range(4):
                    yw[j, c, x4 * 4 + i, pl.ds(8 - R, R), :] = low[pl.ds(R * i, R), :]
                    yw[j, c, x4 * 4 + i, pl.ds(8 + width_y, R), :] = high[pl.ds(R * i, R), :]
            return carry
        lax.fori_loop(0, width_x // 4, unpack, 0)

    def stencil(n, j):
        def body(x, carry):
            potential = pot[x] + (-1.5 * coefficients[0])
            for c in range(2):
                center = tb[n, j, c, x + R]
                total = potential * center
                for k in range(1, R + 1):
                    near = tb[n, j, c, x + R + k] + tb[n, j, c, x + R - k]
                    near = near + (yw[j, c, x, pl.ds(8 + k, width_y), :] + yw[j, c, x, pl.ds(8 - k, width_y), :])
                    near = near + (pltpu.roll(center, k, 1) + pltpu.roll(center, 128 - k, 1))
                    total = total + (-0.5 * coefficients[k]) * near
                stage[j, c, x] = total
            return carry
        lax.fori_loop(0, width_x, body, 0)

    def dots(n):
        for j in range(ORBS):
            for half in range(2):
                ks = range(half * 4, half * 4 + 4)

                def body(x, sums_now):
                    real, imag = tb[n, j, 0, x + R], tb[n, j, 1, x + R]
                    out = []
                    for i, k in enumerate(ks):
                        br, bi = basis[0, k, x], basis[1, k, x]
                        out.append(sums_now[2 * i] + (br * real + bi * imag))
                        out.append(sums_now[2 * i + 1] + (br * imag - bi * real))
                    return tuple(out)
                zero = jnp.zeros((width_y, 128), jnp.float32)
                result = lax.fori_loop(0, width_x, body, (zero,) * 8)
                for i, k in enumerate(ks):
                    rows[pl.ds(16 * j + k, 1), :] = jnp.sum(result[2 * i], axis=0, keepdims=True)
                    rows[pl.ds(16 * j + 8 + k, 1), :] = jnp.sum(result[2 * i + 1], axis=0, keepdims=True)
        ones = jnp.full((8, 128), 1.0 / ncell, jnp.float32)
        line = lax.dot_general(ones, rows[...], (((1,), (1,)), ((), ())), precision=lax.Precision.HIGHEST,
                               preferred_element_type=jnp.float32)
        return line[0:1]

    def reduce_start(n, phase, line):
        peers, ssem, rsem = ((x_peers, a_ssem, a_rsem), (y_peers, b_ssem, b_rsem))[phase]
        msg[n, phase] = line
        copies = []
        for i, peer in enumerate(peers):
            copy = pltpu.make_async_remote_copy(
                src_ref=msg.at[n, phase], dst_ref=sums.at[n, phase, i], send_sem=ssem.at[n, i], recv_sem=rsem.at[n, i],
                device_id=peer, device_id_type=MESH)
            copy.start()
            copies.append(copy)
            pending.append(copy)
        return copies

    def reduce_end(n, phase, copies):
        line = msg[n, phase]
        for i, copy in enumerate(copies):
            copy.wait_recv()
            line = line + sums[n, phase, i]
        return line

    def correct(n, j, line):
        factor = step_size / (n + 1)
        shape = (width_y, 128)
        o_real = [jnp.broadcast_to(line[0:1, 16 * j + k:16 * j + k + 1], shape) for k in range(KCOL)]
        o_imag = [jnp.broadcast_to(line[0:1, 16 * j + 8 + k:16 * j + 9 + k], shape) for k in range(KCOL)]
        last = n == TERMS - 1

        def body(x4, carry):
            packs = ([], [])
            for i in range(4):
                x = x4 * 4 + i
                real, imag = stage[j, 0, x], stage[j, 1, x]
                for k in range(KCOL):
                    br, bi = basis[0, k, x], basis[1, k, x]
                    real = real - (br * o_real[k] - bi * o_imag[k])
                    imag = imag - (br * o_imag[k] + bi * o_real[k])
                t_real, t_imag = factor * imag, -factor * real
                for c, t in ((0, t_real), (1, t_imag)):
                    before = tb[0, j, c, x + R] if n == 0 else acc[j, c, x]
                    acc[j, c, x] = before + t
                    if not last:
                        tb[n + 1, j, c, x + R] = t
                        yw[j, c, x, pl.ds(8, width_y), :] = t
                        packs[c].append(t)
            if not last:
                for c in range(2):
                    pack(n + 1, j, c, x4, packs[c])
            return carry
        lax.fori_loop(0, width_x // 4, body, 0)

    for j in range(ORBS):
        loads[j].wait()

        def first(x4, carry):
            for c in range(2):
                planes = [tb[0, j, c, x4 * 4 + i + R] for i in range(4)]
                for i in range(4):
                    yw[j, c, x4 * 4 + i, pl.ds(8, width_y), :] = planes[i]
                pack(0, j, c, x4, planes)
            return carry
        lax.fori_loop(0, width_x // 4, first, 0)
        if j == 0:
            pl.semaphore_wait(barrier, len(x_peers) + len(y_peers))
        send(0, j)
    loads[2].wait()
    loads[3].wait()
    for n in range(TERMS):
        copies = reduce_start(n, 0, dots(n))
        line = reduce_end(n, 0, copies)
        copies = reduce_start(n, 1, line)
        for j in range(ORBS):
            receive(n, j)
            stencil(n, j)
        line = reduce_end(n, 1, copies)
        for j in range(ORBS):
            correct(n, j, line)
            if n < TERMS - 1:
                send(n + 1, j)
    store = pltpu.make_async_copy(acc, out_hbm, load_sem.at[0])
    store.start()
    for copy in pending:
        copy.wait_send()
    store.wait()


def solution(mesh):
    ngx, ngy = mesh.shape["gx"], mesh.shape["gy"]
    dma = pltpu.SemaphoreType.DMA
    f32 = jnp.float32

    def per_device(psi, basis, potential):
        width_x, width_y, depth = potential.shape
        ncell = width_x * ngx * width_y * ngy * depth
        anywhere = pl.BlockSpec(memory_space=pl.ANY)
        return pl.pallas_call(
            functools.partial(kernel, (ngx, ngy, ncell)),
            out_shape=jax.ShapeDtypeStruct(psi.shape, f32),
            in_specs=[anywhere] * 3,
            out_specs=anywhere,
            scratch_shapes=[
                pltpu.VMEM((TERMS, ORBS, 2, width_x + 2 * R, width_y, depth), f32),
                pltpu.VMEM(basis.shape, f32),
                pltpu.VMEM(potential.shape, f32),
                pltpu.VMEM((ORBS, 2, width_x, 40, depth), f32),
                pltpu.VMEM(psi.shape, f32),
                pltpu.VMEM(psi.shape, f32),
                pltpu.VMEM((TERMS, ORBS, 2, 2 * R * width_x, depth), f32),
                pltpu.VMEM((TERMS, ORBS, 2, 2 * R * width_x, depth), f32),
                pltpu.VMEM((128, depth), f32),
                pltpu.VMEM((TERMS, 2, 1, depth), f32),
                pltpu.VMEM((TERMS, 2, ngy - 1, 1, depth), f32),
                dma((4,)),
                dma((TERMS, ORBS, 2)),
                dma((TERMS, ORBS, 2)),
                dma((TERMS, ORBS, 2)),
                dma((TERMS, ORBS, 2)),
                dma((TERMS, ngx - 1)),
                dma((TERMS, ngx - 1)),
                dma((TERMS, ngy - 1)),
                dma((TERMS, ngy - 1)),
            ],
            compiler_params=pltpu.CompilerParams(
                collective_id=0, has_side_effects=True, vmem_limit_bytes=48 * 2**20),
            name="taylor",
        )(psi, basis, potential)

    placed = (P(None, None, "gx", "gy", None), P(None, None, "gx", "gy", None), P("gx", "gy", None))
    return jax.shard_map(per_device, mesh=mesh, in_specs=placed, out_specs=P(None, None, "gx", "gy", None),
                         check_vma=False)
```

```python
import functools

import jax
import jax.numpy as jnp
import numpy as np
from jax import lax
from jax.experimental import pallas as pl
from jax.experimental.pallas import tpu as pltpu
from jax.sharding import PartitionSpec as P

MESH = pl.DeviceIdType.MESH
coefficients = [
    -5369.0 / 1800.0,
    12.0 / 7.0,
    -15.0 / 56.0,
    10.0 / 189.0,
    -1.0 / 112.0,
    2.0 / 1925.0,
    -1.0 / 16632.0,
]
step_size = 0.25
TERMS = 4
ORBS = 2
KCOL = 8
R = 6
EDGE = 2 * R
TOP = 16
GROUP = 4


def times_i(tile, even):
    return jnp.where(even, -pltpu.roll(tile, 7, 0), pltpu.roll(tile, 1, 0))


def kernel(sizes, psi_hbm, basis_hbm, pot_hbm, result, tb, basis, columns, pot1, pot, stage, split, circle, ysend, yrecv, rows, msg, sums,
           load_sem, x_ssem, x_rsem, y_ssem, y_rsem, a_ssem, a_rsem, b_ssem, b_rsem):
    ngx, ngy, ncell = sizes
    width_x, width_r = psi_hbm.shape[1], psi_hbm.shape[2]
    width_y = width_r // 2
    tiles = width_r // 8
    gx, gy = lax.axis_index("gx"), lax.axis_index("gy")
    x_near = [(lax.rem(gx + d, ngx), gy) for d in (ngx - 1, 1)]
    y_near = [(gx, lax.rem(gy + d, ngy)) for d in (ngy - 1, 1)]
    core, chip = lax.rem(gx, 2), gx // 2
    cy, cz = gy // 4, lax.rem(gy, 4)
    x_peers = [(chip * 2 + 1 - core, gy)]
    steps = sorted(((i, j, k) for i in range(4) for j in range(4) for k in range(4) if i + j + k > 0),
                   key=lambda step: -sum(min(d, 4 - d) for d in step))
    y_peers = [(lax.rem(chip + i, 4) * 2 + core, lax.rem(cy + j, 4) * 4 + lax.rem(cz + k, 4)) for i, j, k in steps]
    inner = pl.ds(TOP, width_r)
    sublane = lax.broadcasted_iota(jnp.int32, (8, 128), 0)
    lane = lax.broadcasted_iota(jnp.int32, (8, 128), 1)
    even = lax.rem(sublane, 2) == 0

    loads = []
    for j in range(ORBS):
        loads.append(pltpu.make_async_copy(psi_hbm.at[j], tb.at[0, j, pl.ds(R, width_x), inner], load_sem.at[j]))
    for part in range(2):
        loads.append(pltpu.make_async_copy(basis_hbm.at[part], basis.at[:, :, part], load_sem.at[2 + part]))
    loads.append(pltpu.make_async_copy(pot_hbm, pot1, load_sem.at[4]))
    for copy in loads:
        copy.start()
    barrier = pltpu.get_barrier_semaphore()
    outer = (lax.rem(gx + 2 * core + ngx - 1, ngx), gy)
    pl.semaphore_signal(barrier, inc=1, device_id=outer, device_id_type=MESH)
    for peer in x_peers + y_peers:
        pl.semaphore_signal(barrier, inc=1, device_id=peer, device_id_type=MESH)

    pending = []

    def pack(n, j, x2, i, low, high):
        base = pl.multiple_of(x2 * 2 * EDGE, 8)
        for side, (first, second) in ((0, low), (1, high)):
            part = ysend.at[n, j, side, pl.ds(base, 2 * EDGE)]
            part[pl.ds(i * EDGE, first.shape[0]), :] = first
            part[pl.ds(i * EDGE + first.shape[0], second.shape[0]), :] = second

    def x_copy(n, j, side):
        src = R if side == 0 else width_x
        dst = width_x + R if side == 0 else 0
        return pltpu.make_async_remote_copy(
            src_ref=tb.at[n, j, pl.ds(src, R), inner], dst_ref=tb.at[n, j, pl.ds(dst, R), inner],
            send_sem=x_ssem.at[n, j, side], recv_sem=x_rsem.at[n, j, 1 - side],
            device_id=x_near[side], device_id_type=MESH)

    def y_copy(n, j, side):
        return pltpu.make_async_remote_copy(
            src_ref=ysend.at[n, j, side], dst_ref=yrecv.at[n, j, 1 - side],
            send_sem=y_ssem.at[n, j, side], recv_sem=y_rsem.at[n, j, 1 - side],
            device_id=y_near[side], device_id_type=MESH)

    def send(make, n, j):
        for side in range(2):
            copy = make(n, j, side)
            copy.start()
            pending.append(copy)

    def receive(n, j):
        for make in (x_copy, y_copy):
            for side in range(2):
                make(n, j, side).wait_recv()

        def unpack(x2, carry):
            base = pl.multiple_of(x2 * 2 * EDGE, 8)
            for side in range(2):
                part = yrecv.at[n, j, side, pl.ds(base, 2 * EDGE)]
                at = TOP - EDGE if side == 0 else TOP + width_r
                for i in range(2):
                    tb[n, j, R + x2 * 2 + i, pl.ds(at, EDGE), :] = part[pl.ds(i * EDGE, EDGE), :]
            return carry
        lax.fori_loop(0, width_x // 2, unpack, 0)

    def along_z(n, j):
        def halves(x2, carry):
            planes = tb[n, j, pl.ds(R + x2 * 2, 2), inner].reshape(2 * width_r, 128)
            high = planes.astype(jnp.bfloat16)
            at = pl.ds(pl.multiple_of(x2 * 2 * width_r, 16), 2 * width_r)
            split[at, 0:128] = high
            split[at, 128:256] = (planes - high.astype(jnp.float32)).astype(jnp.bfloat16)
            return carry
        lax.fori_loop(0, width_x // 2, halves, 0)
        found = jnp.dot(split[...], circle[...], preferred_element_type=jnp.float32)
        stage[j] = (found[:, 0:128] + found[:, 128:256]).reshape(width_x, width_r, 128)

    def along_xy(n, j):
        half = [-0.5 * c for c in coefficients]

        def body(group, carry):
            x0 = group * GROUP
            for r in range(tiles):
                window = [tb[n, j, x0 + i, pl.ds(TOP + 8 * r, 8), :] for i in range(GROUP + 2 * R)]
                for i in range(GROUP):
                    x = x0 + i
                    total = stage[j, x, pl.ds(8 * r, 8), :] + pot[x, pl.ds(8 * r, 8), :] * window[R + i]
                    for k in range(1, R + 1):
                        near = window[R + i + k] + window[R + i - k]
                        near = near + (tb[n, j, R + x, pl.ds(TOP + 8 * r + 2 * k, 8), :]
                                       + tb[n, j, R + x, pl.ds(TOP + 8 * r - 2 * k, 8), :])
                        total = total + half[k] * near
                    stage[j, x, pl.ds(8 * r, 8), :] = total
            return carry
        lax.fori_loop(0, width_x // GROUP, body, 0)

    def dots(n):
        def body(x, carry):
            out = list(carry)
            for y in range(width_y):
                br, bi = basis[x, y, 0], basis[x, y, 1]
                for j in range(ORBS):
                    real = tb[n, j, R + x, pl.ds(TOP + 2 * y, 1), :]
                    imag = tb[n, j, R + x, pl.ds(TOP + 2 * y + 1, 1), :]
                    at = 4 * (y % 2) + 2 * j
                    out[at] = out[at] + (br * real + bi * imag)
                    out[at + 1] = out[at + 1] + (br * imag - bi * real)
            return tuple(out)
        zero = jnp.zeros((8, 128), jnp.float32)
        found = lax.fori_loop(0, width_x, body, (zero,) * 8)
        packed = jnp.zeros((8, 128), jnp.float32)
        for v in range(4):
            summed = jnp.sum(found[v] + found[4 + v], axis=1, keepdims=True)
            packed = jnp.where(lane == 8 * v + sublane, summed, packed)
        return jnp.sum(packed, axis=0, keepdims=True) * (1.0 / ncell)

    def reduce_start(n, phase, line):
        peers, ssem, rsem = ((x_peers, a_ssem, a_rsem), (y_peers, b_ssem, b_rsem))[phase]
        msg[n, phase] = line
        for i, peer in enumerate(peers):
            pltpu.make_async_remote_copy(
                src_ref=msg.at[n, phase], dst_ref=sums.at[n, phase, i], send_sem=ssem.at[n], recv_sem=rsem.at[n],
                device_id=peer, device_id_type=MESH).start()

    def reduce_wait(n, phase, sem):
        count = len((x_peers, y_peers)[phase])
        every = sums.at[n, phase, pl.ds(0, count)]
        pltpu.make_async_copy(every, every, sem.at[n]).wait()
        return count

    def reduce_end(n, phase):
        count = reduce_wait(n, phase, (a_rsem, b_rsem)[phase])
        parts = [msg[n, phase]] + [sums[n, phase, i] for i in range(count)]
        while len(parts) > 1:
            parts = [sum(parts[i:i + 2][1:], parts[i]) for i in range(0, len(parts), 2)]
        return parts[0]

    def unpack_line(line):
        whole = jnp.broadcast_to(line, (8, 128))
        for v in range(4):
            own = jnp.where(lane == 8 * v + sublane, whole, 0.0)
            rows[pl.ds(8 * v, 8), :] = jnp.broadcast_to(jnp.sum(own, axis=1, keepdims=True), (8, 128))

    def correct(n, j):
        factor = step_size / (n + 1)
        o_real = [jnp.broadcast_to(rows[pl.ds(16 * j + k, 1), :], (8, 128)) for k in range(KCOL)]
        o_imag = [jnp.broadcast_to(rows[pl.ds(16 * j + 8 + k, 1), :], (8, 128)) for k in range(KCOL)]
        last = n == TERMS - 1

        def body(x2, carry):
            for i in range(2):
                x = x2 * 2 + i
                out = []
                for r in range(tiles):
                    along = jnp.zeros((8, 128), jnp.float32)
                    across = jnp.zeros((8, 128), jnp.float32)
                    for k in range(KCOL):
                        column = columns[k, x, pl.ds(8 * r, 8), :]
                        along = along + column * o_real[k]
                        across = across + column * o_imag[k]
                    total = stage[j, x, pl.ds(8 * r, 8), :] - along - times_i(across, even)
                    out.append(factor * total)
                if not last:
                    for r in range(tiles):
                        tb[n + 1, j, R + x, pl.ds(TOP + 8 * r, 8), :] = out[r]
                    pack(n + 1, j, x2, i, (out[0], out[1][0:4]), (out[3][4:8], out[4]))
                else:
                    for r in range(tiles):
                        t = [tb[m, j, R + x, pl.ds(TOP + 8 * r, 8), :] for m in range(TERMS)]
                        result[j, x, pl.ds(8 * r, 8), :] = (t[0] - t[2] + out[r]) - times_i(t[1] - t[3], even)
            return carry
        lax.fori_loop(0, width_x // 2, body, 0)

    offset = lax.rem(lax.broadcasted_iota(jnp.int32, (128, 128), 0) - lax.broadcasted_iota(jnp.int32, (128, 128), 1) + 128, 128)
    high = jnp.zeros((128, 128), jnp.float32)
    low = jnp.zeros((128, 128), jnp.float32)
    for k in range(1, R + 1):
        value = np.float32(-0.5 * coefficients[k])
        first = np.float32(value.astype(jnp.bfloat16))
        here = (offset == k) | (offset == 128 - k)
        high = jnp.where(here, first, high)
        low = jnp.where(here, np.float32(value - first), low)
    for side in range(2):
        circle[pl.ds(128 * side, 128), 0:128] = high.astype(jnp.bfloat16)
        circle[pl.ds(128 * side, 128), 128:256] = low.astype(jnp.bfloat16)

    for j in range(ORBS):
        loads[j].wait()

        def first(x2, carry):
            for i in range(2):
                t = [tb[0, j, R + x2 * 2 + i, pl.ds(TOP + 8 * r, 8), :] for r in (0, 1, 3, 4)]
                pack(0, j, x2, i, (t[0], t[1][0:4]), (t[2][4:8], t[3]))
            return carry
        lax.fori_loop(0, width_x // 2, first, 0)
        if j == 0:
            pl.semaphore_wait(barrier, len(x_peers) + len(y_peers) + 1)
        send(y_copy, 0, j)
        if j == 0:
            send(x_copy, 0, j)
    loads[2].wait()
    loads[3].wait()
    for n in range(TERMS):
        reduce_start(n, 0, dots(n))
        send(x_copy, n, 1)
        if n == 0:
            loads[4].wait()

            def spread(x, carry):
                plane = pot1[x] + (-1.5 * coefficients[0])
                for part in range(2):
                    pot[x, pl.ds(part, width_y, stride=2), :] = plane
                for r in range(tiles):
                    here = basis.at[x, pl.ds(4 * r, 4)].reshape(64, 128)
                    for k in range(KCOL):
                        columns[k, x, pl.ds(8 * r, 8), :] = here[pl.ds(k, 8, stride=8), :]
                return carry
            lax.fori_loop(0, width_x, spread, 0)
        for j in range(ORBS):
            along_z(n, j)
        reduce_start(n, 1, reduce_end(n, 0))
        for j in range(ORBS):
            receive(n, j)
            along_xy(n, j)
        unpack_line(reduce_end(n, 1))
        for j in range(ORBS):
            correct(n, j)
            if n < TERMS - 1:
                send(y_copy, n + 1, j)
                if j == 0:
                    send(x_copy, n + 1, j)
    for copy in pending:
        copy.wait_send()
    for n in range(TERMS):
        reduce_wait(n, 0, a_ssem)
        reduce_wait(n, 1, b_ssem)


def solution(mesh):
    ngx, ngy = mesh.shape["gx"], mesh.shape["gy"]
    dma = pltpu.SemaphoreType.DMA
    f32, bf16 = jnp.float32, jnp.bfloat16

    def per_device(psi, basis, potential):
        width_x, width_y, depth = potential.shape
        ncell = width_x * ngx * width_y * ngy * depth
        far = pl.BlockSpec(memory_space=pltpu.HBM)
        psi = psi.transpose(0, 2, 3, 1, 4).reshape(ORBS, width_x, 2 * width_y, depth)
        basis = basis.transpose(0, 2, 3, 1, 4)
        out = pl.pallas_call(
            functools.partial(kernel, (ngx, ngy, ncell)),
            out_shape=pltpu.VMEM(psi.shape, f32),
            in_specs=[far] * 3,
            out_specs=pl.BlockSpec(memory_space=pltpu.VMEM),
            scratch_shapes=[
                pltpu.VMEM((TERMS, ORBS, width_x + 2 * R, 72, depth), f32),
                pltpu.VMEM((width_x, width_y, 2, KCOL, depth), f32),
                pltpu.VMEM((KCOL, width_x, 2 * width_y, depth), f32),
                pltpu.VMEM((width_x, width_y, depth), f32),
                pltpu.VMEM((width_x, 2 * width_y, depth), f32),
                pltpu.VMEM(psi.shape, f32),
                pltpu.VMEM((2 * width_x * width_y, 2 * depth), bf16),
                pltpu.VMEM((2 * depth, 2 * depth), bf16),
                pltpu.VMEM((TERMS, ORBS, 2, EDGE * width_x, depth), f32),
                pltpu.VMEM((TERMS, ORBS, 2, EDGE * width_x, depth), f32),
                pltpu.VMEM((32, depth), f32),
                pltpu.VMEM((TERMS, 2, 1, depth), f32),
                pltpu.VMEM((TERMS, 2, 63, 1, depth), f32),
                dma((5,)),
                dma((TERMS, ORBS, 2)),
                dma((TERMS, ORBS, 2)),
                dma((TERMS, ORBS, 2)),
                dma((TERMS, ORBS, 2)),
                dma((TERMS,)),
                dma((TERMS,)),
                dma((TERMS,)),
                dma((TERMS,)),
            ],
            compiler_params=pltpu.CompilerParams(
                collective_id=0, has_side_effects=True, vmem_limit_bytes=60 * 2**20),
            name="taylor",
        )(psi, basis, potential)
        return out.reshape(ORBS, width_x, width_y, 2, depth).transpose(0, 3, 1, 2, 4)

    placed = (P(None, None, "gx", "gy", None), P(None, None, "gx", "gy", None), P("gx", "gy", None))
    return jax.shard_map(per_device, mesh=mesh, in_specs=placed, out_specs=P(None, None, "gx", "gy", None),
                         check_vma=False)
```

```python
import functools

import jax
import jax.numpy as jnp
import numpy as np
from jax import lax
from jax.experimental import pallas as pl
from jax.experimental.pallas import tpu as pltpu
from jax.sharding import PartitionSpec as P

MESH = pl.DeviceIdType.MESH
coefficients = [
    -5369.0 / 1800.0,
    12.0 / 7.0,
    -15.0 / 56.0,
    10.0 / 189.0,
    -1.0 / 112.0,
    2.0 / 1925.0,
    -1.0 / 16632.0,
]
step_size = 0.25
TERMS = 4
ORBS = 2
KCOL = 8
R = 6
EDGE = 2 * R
HALVES = 2
TOP = 16
GROUP = 4


def times_i(tile, even):
    return jnp.where(even, -pltpu.roll(tile, 7, 0), pltpu.roll(tile, 1, 0))


def kernel(sizes, psi_hbm, basis_hbm, pot_hbm, result, tb, basis, columns, pot1, pot, stage, split, circle, ysend, yrecv, rows, msg, sums,
           load_sem, x_ssem, x_rsem, y_ssem, y_rsem, a_ssem, a_rsem, b_ssem, b_rsem):
    ngx, ngy, ncell = sizes
    width_x, width_r = psi_hbm.shape[1], psi_hbm.shape[2]
    width_y = width_r // 2
    tiles = width_r // 8
    gx, gy = lax.axis_index("gx"), lax.axis_index("gy")
    x_near = [(lax.rem(gx + d, ngx), gy) for d in (ngx - 1, 1)]
    y_near = [(gx, lax.rem(gy + d, ngy)) for d in (ngy - 1, 1)]
    core, chip = lax.rem(gx, 2), gx // 2
    cy, cz = gy // 4, lax.rem(gy, 4)
    x_peers = [(chip * 2 + 1 - core, gy)]
    steps = sorted(((i, j, k) for i in range(4) for j in range(4) for k in range(4) if i + j + k > 0),
                   key=lambda step: -sum(min(d, 4 - d) for d in step))
    y_peers = [(lax.rem(chip + i, 4) * 2 + core, lax.rem(cy + j, 4) * 4 + lax.rem(cz + k, 4)) for i, j, k in steps]
    inner = pl.ds(TOP, width_r)
    sublane = lax.broadcasted_iota(jnp.int32, (8, 128), 0)
    lane = lax.broadcasted_iota(jnp.int32, (8, 128), 1)
    even = lax.rem(sublane, 2) == 0

    loads = []
    for j in range(ORBS):
        loads.append(pltpu.make_async_copy(psi_hbm.at[j], tb.at[0, j, pl.ds(R, width_x), inner], load_sem.at[j]))
    for part in range(2):
        loads.append(pltpu.make_async_copy(basis_hbm.at[part], basis.at[:, :, part], load_sem.at[2 + part]))
    loads.append(pltpu.make_async_copy(pot_hbm, pot1, load_sem.at[4]))
    for copy in loads:
        copy.start()
    barrier = pltpu.get_barrier_semaphore()
    outer = (lax.rem(gx + 2 * core + ngx - 1, ngx), gy)
    pl.semaphore_signal(barrier, inc=1, device_id=outer, device_id_type=MESH)
    for peer in x_peers + y_peers:
        pl.semaphore_signal(barrier, inc=1, device_id=peer, device_id_type=MESH)

    pending = []

    def pack(n, j, x2, i, low, high):
        base = pl.multiple_of(x2 * 2 * EDGE, 8)
        for side, (first, second) in ((0, low), (1, high)):
            part = ysend.at[n, j, side, pl.ds(base, 2 * EDGE)]
            part[pl.ds(i * EDGE, first.shape[0]), :] = first
            part[pl.ds(i * EDGE + first.shape[0], second.shape[0]), :] = second

    def x_copy(n, j, side):
        src = R if side == 0 else width_x
        dst = width_x + R if side == 0 else 0
        return pltpu.make_async_remote_copy(
            src_ref=tb.at[n, j, pl.ds(src, R), inner], dst_ref=tb.at[n, j, pl.ds(dst, R), inner],
            send_sem=x_ssem.at[n, j, side], recv_sem=x_rsem.at[n, j, 1 - side],
            device_id=x_near[side], device_id_type=MESH)

    def y_copy(n, j, side, part):
        depth = EDGE * width_x // HALVES
        at = pl.ds(part * depth, depth)
        return pltpu.make_async_remote_copy(
            src_ref=ysend.at[n, j, side, at], dst_ref=yrecv.at[n, j, 1 - side, at],
            send_sem=y_ssem.at[n, j, side, part], recv_sem=y_rsem.at[n, j, 1 - side, part],
            device_id=y_near[side], device_id_type=MESH)

    def send(make, *key, sides=(0, 1)):
        for side in sides:
            copy = make(key[0], key[1], side, *key[2:])
            copy.start()
            pending.append(copy)

    def receive_x(n, j):
        for side in range(2):
            x_copy(n, j, side).wait_recv()

    def receive_y(n, j, part):
        for side in range(2):
            y_copy(n, j, side, part).wait_recv()

        def unpack(x2, carry):
            base = pl.multiple_of(x2 * 2 * EDGE, 8)
            for side in range(2):
                rim = yrecv.at[n, j, side, pl.ds(base, 2 * EDGE)]
                at = TOP - EDGE if side == 0 else TOP + width_r
                for i in range(2):
                    tb[n, j, R + x2 * 2 + i, pl.ds(at, EDGE), :] = rim[pl.ds(i * EDGE, EDGE), :]
            return carry
        lax.fori_loop(part * (width_x // 2 // HALVES), (part + 1) * (width_x // 2 // HALVES), unpack, 0)

    def along_z(n, j):
        def halves(x2, carry):
            planes = tb[n, j, pl.ds(R + x2 * 2, 2), inner].reshape(2 * width_r, 128)
            high = planes.astype(jnp.bfloat16)
            at = pl.ds(pl.multiple_of(x2 * 2 * width_r, 16), 2 * width_r)
            split[at, 0:128] = high
            split[at, 128:256] = (planes - high.astype(jnp.float32)).astype(jnp.bfloat16)
            return carry
        lax.fori_loop(0, width_x // 2, halves, 0)
        found = jnp.dot(split[...], circle[...], preferred_element_type=jnp.float32)
        stage[j] = (found[:, 0:128] + found[:, 128:256]).reshape(width_x, width_r, 128)

    half = [-0.5 * c for c in coefficients]

    def along_x(n, j):
        def body(group, carry):
            x0 = group * GROUP
            for r in range(tiles):
                window = [tb[n, j, x0 + i, pl.ds(TOP + 8 * r, 8), :] for i in range(GROUP + 2 * R)]
                for i in range(GROUP):
                    x = x0 + i
                    total = stage[j, x, pl.ds(8 * r, 8), :] + pot[x, pl.ds(8 * r, 8), :] * window[R + i]
                    for k in range(1, R + 1):
                        total = total + half[k] * (window[R + i + k] + window[R + i - k])
                    stage[j, x, pl.ds(8 * r, 8), :] = total
            return carry
        lax.fori_loop(0, width_x // GROUP, body, 0)

    def along_y(n, j, part):
        def body(x, carry):
            for r in range(tiles):
                total = stage[j, x, pl.ds(8 * r, 8), :]
                for k in range(1, R + 1):
                    near = tb[n, j, R + x, pl.ds(TOP + 8 * r + 2 * k, 8), :]
                    near = near + tb[n, j, R + x, pl.ds(TOP + 8 * r - 2 * k, 8), :]
                    total = total + half[k] * near
                stage[j, x, pl.ds(8 * r, 8), :] = total
            return carry
        lax.fori_loop(part * (width_x // HALVES), (part + 1) * (width_x // HALVES), body, 0, unroll=2)

    def dots(field, j, first_x, first_row, low, high):
        def body(x, carry):
            out = list(carry)
            for y in range(width_y):
                br, bi = basis[x, y, 0], basis[x, y, 1]
                real = field[j, first_x + x, pl.ds(first_row + 2 * y, 1), :]
                imag = field[j, first_x + x, pl.ds(first_row + 2 * y + 1, 1), :]
                at = 2 * (y % 2)
                out[at] = out[at] + (br * real + bi * imag)
                out[at + 1] = out[at + 1] + (br * imag - bi * real)
            return tuple(out)
        zero = jnp.zeros((8, 128), jnp.float32)
        found = lax.fori_loop(low, high, body, (zero,) * 4)
        return [(found[i] + found[2 + i]) * (1.0 / ncell) for i in range(2)]

    def pack_line(vectors):
        packed = jnp.zeros((8, 128), jnp.float32)
        for v, vector in enumerate(vectors):
            packed = jnp.where(lane == 8 * v + sublane, jnp.sum(vector, axis=1, keepdims=True), packed)
        return jnp.sum(packed, axis=0, keepdims=True)

    def reduce_start(n, phase, line):
        peers, ssem, rsem = ((x_peers, a_ssem, a_rsem), (y_peers, b_ssem, b_rsem))[phase]
        msg[n, phase] = line
        for i, peer in enumerate(peers):
            pltpu.make_async_remote_copy(
                src_ref=msg.at[n, phase], dst_ref=sums.at[n, phase, i], send_sem=ssem.at[n], recv_sem=rsem.at[n],
                device_id=peer, device_id_type=MESH).start()

    def reduce_wait(n, phase, sem):
        count = len((x_peers, y_peers)[phase])
        every = sums.at[n, phase, pl.ds(0, count)]
        pltpu.make_async_copy(every, every, sem.at[n]).wait()
        return count

    def reduce_end(n, phase):
        count = reduce_wait(n, phase, (a_rsem, b_rsem)[phase])
        parts = [msg[n, phase]] + [sums[n, phase, i] for i in range(count)]
        while len(parts) > 1:
            parts = [sum(parts[i:i + 2][1:], parts[i]) for i in range(0, len(parts), 2)]
        return parts[0]

    def unpack_line(line):
        whole = jnp.broadcast_to(line, (8, 128))
        for v in range(4):
            own = jnp.where(lane == 8 * v + sublane, whole, 0.0)
            rows[pl.ds(8 * v, 8), :] = jnp.broadcast_to(jnp.sum(own, axis=1, keepdims=True), (8, 128))

    def correct(n, j, part):
        factor = step_size / (n + 1)
        o_real = [jnp.broadcast_to(rows[pl.ds(16 * j + k, 1), :], (8, 128)) for k in range(KCOL)]
        o_imag = [jnp.broadcast_to(rows[pl.ds(16 * j + 8 + k, 1), :], (8, 128)) for k in range(KCOL)]
        last = n == TERMS - 1

        def body(x2, carry):
            for i in range(2):
                x = x2 * 2 + i
                out = []
                for r in range(tiles):
                    along = jnp.zeros((8, 128), jnp.float32)
                    across = jnp.zeros((8, 128), jnp.float32)
                    for k in range(KCOL):
                        column = columns[k, x, pl.ds(8 * r, 8), :]
                        along = along + column * o_real[k]
                        across = across + column * o_imag[k]
                    total = stage[j, x, pl.ds(8 * r, 8), :] - along - times_i(across, even)
                    out.append(factor * total)
                if not last:
                    for r in range(tiles):
                        tb[n + 1, j, R + x, pl.ds(TOP + 8 * r, 8), :] = out[r]
                    pack(n + 1, j, x2, i, (out[0], out[1][0:4]), (out[3][4:8], out[4]))
                else:
                    for r in range(tiles):
                        result[j, x, pl.ds(8 * r, 8), :] = result[j, x, pl.ds(8 * r, 8), :] + out[r]
            return carry
        lax.fori_loop(part * (width_x // 2 // HALVES), (part + 1) * (width_x // 2 // HALVES), body, 0)

    def combine(j):
        def body(x, carry):
            for r in range(tiles):
                t = [tb[m, j, R + x, pl.ds(TOP + 8 * r, 8), :] for m in range(TERMS)]
                result[j, x, pl.ds(8 * r, 8), :] = (t[0] - t[2]) - times_i(t[1] - t[3], even)
            return carry
        lax.fori_loop(0, width_x, body, 0)

    offset = lax.rem(lax.broadcasted_iota(jnp.int32, (128, 128), 0) - lax.broadcasted_iota(jnp.int32, (128, 128), 1) + 128, 128)
    high = jnp.zeros((128, 128), jnp.float32)
    low = jnp.zeros((128, 128), jnp.float32)
    for k in range(1, R + 1):
        value = np.float32(-0.5 * coefficients[k])
        first = np.float32(value.astype(jnp.bfloat16))
        here = (offset == k) | (offset == 128 - k)
        high = jnp.where(here, first, high)
        low = jnp.where(here, np.float32(value - first), low)
    for side in range(2):
        circle[pl.ds(128 * side, 128), 0:128] = high.astype(jnp.bfloat16)
        circle[pl.ds(128 * side, 128), 128:256] = low.astype(jnp.bfloat16)

    for j in range(ORBS):
        loads[j].wait()

        def first(x2, carry):
            for i in range(2):
                t = [tb[0, j, R + x2 * 2 + i, pl.ds(TOP + 8 * r, 8), :] for r in (0, 1, 3, 4)]
                pack(0, j, x2, i, (t[0], t[1][0:4]), (t[2][4:8], t[3]))
            return carry
        lax.fori_loop(0, width_x // 2, first, 0)
        if j == 0:
            pl.semaphore_wait(barrier, len(x_peers) + len(y_peers) + 1)
        for part in range(HALVES):
            send(y_copy, 0, j, part)
        if j == 0:
            send(x_copy, 0, j)
    loads[2].wait()
    loads[3].wait()
    start = []
    for j in range(ORBS):
        start = start + dots(tb.at[0], j, R, TOP, 0, width_x)
    reduce_start(0, 0, pack_line(start))
    send(x_copy, 0, 1)
    loads[4].wait()

    def spread(x, carry):
        plane = pot1[x] + (-1.5 * coefficients[0])
        for part in range(2):
            pot[x, pl.ds(part, width_y, stride=2), :] = plane
        for r in range(tiles):
            here = basis.at[x, pl.ds(4 * r, 4)].reshape(64, 128)
            for k in range(KCOL):
                columns[k, x, pl.ds(8 * r, 8), :] = here[pl.ds(k, 8, stride=8), :]
        return carry

    for n in range(TERMS):
        reduce_start(n, 1, reduce_end(n, 0))
        if n == 0:
            lax.fori_loop(0, width_x, spread, 0)
        for j in range(ORBS):
            along_z(n, j)
        for j in range(ORBS):
            receive_x(n, j)
            along_x(n, j)
            for part in range(HALVES):
                receive_y(n, j, part)
                along_y(n, j, part)
        if n == TERMS - 1:
            for j in range(ORBS):
                combine(j)
        line = reduce_end(n, 1)
        unpack_line(line)
        for j in range(ORBS):
            for part in range(HALVES):
                correct(n, j, part)
                if n < TERMS - 1:
                    send(y_copy, n + 1, j, part)
                    send(x_copy, n + 1, j, sides=(part,))
        if n < TERMS - 1:
            start = []
            for j in range(ORBS):
                start = start + dots(tb.at[n + 1], j, R, TOP, 0, width_x)
            reduce_start(n + 1, 0, pack_line(start))
    for copy in pending:
        copy.wait_send()
    for n in range(TERMS):
        reduce_wait(n, 0, a_ssem)
        reduce_wait(n, 1, b_ssem)


def solution(mesh):
    ngx, ngy = mesh.shape["gx"], mesh.shape["gy"]
    dma = pltpu.SemaphoreType.DMA
    f32, bf16 = jnp.float32, jnp.bfloat16

    def per_device(psi, basis, potential):
        width_x, width_y, depth = potential.shape
        ncell = width_x * ngx * width_y * ngy * depth
        far = pl.BlockSpec(memory_space=pltpu.HBM)
        psi = psi.transpose(0, 2, 3, 1, 4).reshape(ORBS, width_x, 2 * width_y, depth)
        basis = basis.transpose(0, 2, 3, 1, 4)
        out = pl.pallas_call(
            functools.partial(kernel, (ngx, ngy, ncell)),
            out_shape=pltpu.VMEM(psi.shape, f32),
            in_specs=[far] * 3,
            out_specs=pl.BlockSpec(memory_space=pltpu.VMEM),
            scratch_shapes=[
                pltpu.VMEM((TERMS, ORBS, width_x + 2 * R, 72, depth), f32),
                pltpu.VMEM((width_x, width_y, 2, KCOL, depth), f32),
                pltpu.VMEM((KCOL, width_x, 2 * width_y, depth), f32),
                pltpu.VMEM((width_x, width_y, depth), f32),
                pltpu.VMEM((width_x, 2 * width_y, depth), f32),
                pltpu.VMEM(psi.shape, f32),
                pltpu.VMEM((2 * width_x * width_y, 2 * depth), bf16),
                pltpu.VMEM((2 * depth, 2 * depth), bf16),
                pltpu.VMEM((TERMS, ORBS, 2, EDGE * width_x, depth), f32),
                pltpu.VMEM((TERMS, ORBS, 2, EDGE * width_x, depth), f32),
                pltpu.VMEM((32, depth), f32),
                pltpu.VMEM((TERMS, 2, 1, depth), f32),
                pltpu.VMEM((TERMS, 2, 63, 1, depth), f32),
                dma((5,)),
                dma((TERMS, ORBS, 2)),
                dma((TERMS, ORBS, 2)),
                dma((TERMS, ORBS, 2, HALVES)),
                dma((TERMS, ORBS, 2, HALVES)),
                dma((TERMS,)),
                dma((TERMS,)),
                dma((TERMS,)),
                dma((TERMS,)),
            ],
            compiler_params=pltpu.CompilerParams(
                collective_id=0, has_side_effects=True, vmem_limit_bytes=60 * 2**20),
            name="taylor",
        )(psi, basis, potential)
        return out.reshape(ORBS, width_x, width_y, 2, depth).transpose(0, 3, 1, 2, 4)

    placed = (P(None, None, "gx", "gy", None), P(None, None, "gx", "gy", None), P("gx", "gy", None))
    return jax.shard_map(per_device, mesh=mesh, in_specs=placed, out_specs=P(None, None, "gx", "gy", None),
                         check_vma=False)
```

```python
import functools

import jax
import jax.numpy as jnp
import numpy as np
from jax import lax
from jax.experimental import pallas as pl
from jax.experimental.pallas import tpu as pltpu
from jax.sharding import PartitionSpec as P

MESH = pl.DeviceIdType.MESH
coefficients = [
    -5369.0 / 1800.0,
    12.0 / 7.0,
    -15.0 / 56.0,
    10.0 / 189.0,
    -1.0 / 112.0,
    2.0 / 1925.0,
    -1.0 / 16632.0,
]
step_size = 0.25
TERMS = 4
ORBS = 2
KCOL = 8
R = 6
EDGE = 2 * R
HALVES = 2
TOP = 16
GROUP = 4


def times_i(tile, even):
    return jnp.where(even, -pltpu.roll(tile, 7, 0), pltpu.roll(tile, 1, 0))


def kernel(sizes, psi_hbm, basis_hbm, pot_hbm, result, tb, basis, columns, pot1, pot, stage, split, circle, ysend, yrecv, rows, msg, sums,
           load_sem, x_ssem, x_rsem, y_ssem, y_rsem, a_ssem, a_rsem, b_ssem, b_rsem):
    ngx, ngy, ncell = sizes
    width_x, width_r = psi_hbm.shape[1], psi_hbm.shape[2]
    width_y = width_r // 2
    tiles = width_r // 8
    gx, gy = lax.axis_index("gx"), lax.axis_index("gy")
    x_near = [(lax.rem(gx + d, ngx), gy) for d in (ngx - 1, 1)]
    y_near = [(gx, lax.rem(gy + d, ngy)) for d in (ngy - 1, 1)]
    core, chip = lax.rem(gx, 2), gx // 2
    cy, cz = gy // 4, lax.rem(gy, 4)
    x_peers = [(chip * 2 + 1 - core, gy)]
    steps = sorted(((i, j, k) for i in range(4) for j in range(4) for k in range(4) if i + j + k > 0),
                   key=lambda step: -sum(min(d, 4 - d) for d in step))
    y_peers = [(lax.rem(chip + i, 4) * 2 + core, lax.rem(cy + j, 4) * 4 + lax.rem(cz + k, 4)) for i, j, k in steps]
    gx_peers = [(lax.rem(gx + i, ngx), gy) for i in range(1, ngx)]
    gy_peers = [(gx, lax.rem(gy + i, ngy)) for i in sorted(range(1, ngy), key=lambda i: -min(i % 4, 4 - i % 4) - min(i // 4, 4 - i // 4))]

    def peers_of(n, phase):
        return (gx_peers, gy_peers)[phase] if n == 0 else (x_peers, y_peers)[phase]

    inner = pl.ds(TOP, width_r)
    sublane = lax.broadcasted_iota(jnp.int32, (8, 128), 0)
    lane = lax.broadcasted_iota(jnp.int32, (8, 128), 1)
    even = lax.rem(sublane, 2) == 0

    loads = []
    for j in range(ORBS):
        loads.append(pltpu.make_async_copy(psi_hbm.at[j], tb.at[0, j, pl.ds(R, width_x), inner], load_sem.at[j]))
    for part in range(2):
        loads.append(pltpu.make_async_copy(basis_hbm.at[part], basis.at[:, :, part], load_sem.at[2 + part]))
    loads.append(pltpu.make_async_copy(pot_hbm, pot1, load_sem.at[4]))
    for copy in loads:
        copy.start()
    barrier = pltpu.get_barrier_semaphore()
    for peer in gx_peers + gy_peers:
        pl.semaphore_signal(barrier, inc=1, device_id=peer, device_id_type=MESH)

    pending = []

    def pack(n, j, x2, i, low, high):
        base = pl.multiple_of(x2 * 2 * EDGE, 8)
        for side, (first, second) in ((0, low), (1, high)):
            part = ysend.at[n, j, side, pl.ds(base, 2 * EDGE)]
            part[pl.ds(i * EDGE, first.shape[0]), :] = first
            part[pl.ds(i * EDGE + first.shape[0], second.shape[0]), :] = second

    def x_copy(n, j, side):
        src = R if side == 0 else width_x
        dst = width_x + R if side == 0 else 0
        return pltpu.make_async_remote_copy(
            src_ref=tb.at[n, j, pl.ds(src, R), inner], dst_ref=tb.at[n, j, pl.ds(dst, R), inner],
            send_sem=x_ssem.at[n, j, side], recv_sem=x_rsem.at[n, j, 1 - side],
            device_id=x_near[side], device_id_type=MESH)

    def y_copy(n, j, side, part):
        depth = EDGE * width_x // HALVES
        at = pl.ds(part * depth, depth)
        return pltpu.make_async_remote_copy(
            src_ref=ysend.at[n, j, side, at], dst_ref=yrecv.at[n, j, 1 - side, at],
            send_sem=y_ssem.at[n, j, side, part], recv_sem=y_rsem.at[n, j, 1 - side, part],
            device_id=y_near[side], device_id_type=MESH)

    def send(make, *key, sides=(0, 1)):
        for side in sides:
            copy = make(key[0], key[1], side, *key[2:])
            copy.start()
            pending.append(copy)

    def receive_x(n, j):
        for side in range(2):
            x_copy(n, j, side).wait_recv()

    def receive_y(n, j, part):
        for side in range(2):
            y_copy(n, j, side, part).wait_recv()

        def unpack(x2, carry):
            base = pl.multiple_of(x2 * 2 * EDGE, 8)
            for side in range(2):
                rim = yrecv.at[n, j, side, pl.ds(base, 2 * EDGE)]
                at = TOP - EDGE if side == 0 else TOP + width_r
                for i in range(2):
                    tb[n, j, R + x2 * 2 + i, pl.ds(at, EDGE), :] = rim[pl.ds(i * EDGE, EDGE), :]
            return carry
        lax.fori_loop(part * (width_x // 2 // HALVES), (part + 1) * (width_x // 2 // HALVES), unpack, 0)

    def along_z(n, j):
        def halves(x2, carry):
            planes = tb[n, j, pl.ds(R + x2 * 2, 2), inner].reshape(2 * width_r, 128)
            high = planes.astype(jnp.bfloat16)
            at = pl.ds(pl.multiple_of(x2 * 2 * width_r, 16), 2 * width_r)
            split[at, 0:128] = high
            split[at, 128:256] = (planes - high.astype(jnp.float32)).astype(jnp.bfloat16)
            return carry
        lax.fori_loop(0, width_x // 2, halves, 0)
        found = jnp.dot(split[...], circle[...], preferred_element_type=jnp.float32)
        stage[j] = (found[:, 0:128] + found[:, 128:256]).reshape(width_x, width_r, 128)

    half = [-0.5 * c for c in coefficients]

    def along_x(n, j):
        def body(group, carry):
            x0 = group * GROUP
            for r in range(tiles):
                window = [tb[n, j, x0 + i, pl.ds(TOP + 8 * r, 8), :] for i in range(GROUP + 2 * R)]
                for i in range(GROUP):
                    x = x0 + i
                    total = stage[j, x, pl.ds(8 * r, 8), :] + pot[x, pl.ds(8 * r, 8), :] * window[R + i]
                    for k in range(1, R + 1):
                        total = total + half[k] * (window[R + i + k] + window[R + i - k])
                    stage[j, x, pl.ds(8 * r, 8), :] = total
            return carry
        lax.fori_loop(0, width_x // GROUP, body, 0)

    def along_y(n, j, part):
        def body(x, carry):
            for r in range(tiles):
                total = stage[j, x, pl.ds(8 * r, 8), :]
                for k in range(1, R + 1):
                    near = tb[n, j, R + x, pl.ds(TOP + 8 * r + 2 * k, 8), :]
                    near = near + tb[n, j, R + x, pl.ds(TOP + 8 * r - 2 * k, 8), :]
                    total = total + half[k] * near
                stage[j, x, pl.ds(8 * r, 8), :] = total
            return carry
        lax.fori_loop(part * (width_x // HALVES), (part + 1) * (width_x // HALVES), body, 0, unroll=2)

    def dots(field, j, first_x, first_row, low, high):
        def body(x, carry):
            out = list(carry)
            for y in range(width_y):
                br, bi = basis[x, y, 0], basis[x, y, 1]
                real = field[j, first_x + x, pl.ds(first_row + 2 * y, 1), :]
                imag = field[j, first_x + x, pl.ds(first_row + 2 * y + 1, 1), :]
                at = 2 * (y % 2)
                out[at] = out[at] + (br * real + bi * imag)
                out[at + 1] = out[at + 1] + (br * imag - bi * real)
            return tuple(out)
        zero = jnp.zeros((8, 128), jnp.float32)
        found = lax.fori_loop(low, high, body, (zero,) * 4)
        return [(found[i] + found[2 + i]) * (1.0 / ncell) for i in range(2)]

    def pack_line(vectors):
        packed = jnp.zeros((8, 128), jnp.float32)
        for v, vector in enumerate(vectors):
            packed = jnp.where(lane == 8 * v + sublane, jnp.sum(vector, axis=1, keepdims=True), packed)
        return jnp.sum(packed, axis=0, keepdims=True)

    def reduce_start(n, phase, line):
        ssem, rsem = ((a_ssem, a_rsem), (b_ssem, b_rsem))[phase]
        msg[n, phase] = line
        for i, peer in enumerate(peers_of(n, phase)):
            pltpu.make_async_remote_copy(
                src_ref=msg.at[n, phase], dst_ref=sums.at[n, phase, i], send_sem=ssem.at[n], recv_sem=rsem.at[n],
                device_id=peer, device_id_type=MESH).start()

    def reduce_wait(n, phase, sem):
        count = len(peers_of(n, phase))
        every = sums.at[n, phase, pl.ds(0, count)]
        pltpu.make_async_copy(every, every, sem.at[n]).wait()
        return count

    def reduce_end(n, phase):
        count = reduce_wait(n, phase, (a_rsem, b_rsem)[phase])
        parts = [msg[n, phase]] + [sums[n, phase, i] for i in range(count)]
        while len(parts) > 1:
            parts = [sum(parts[i:i + 2][1:], parts[i]) for i in range(0, len(parts), 2)]
        return parts[0]

    def unpack_line(line):
        whole = jnp.broadcast_to(line, (8, 128))
        for v in range(4):
            own = jnp.where(lane == 8 * v + sublane, whole, 0.0)
            rows[pl.ds(8 * v, 8), :] = jnp.broadcast_to(jnp.sum(own, axis=1, keepdims=True), (8, 128))

    def correct(n, j, part):
        factor = step_size / (n + 1)
        o_real = [jnp.broadcast_to(rows[pl.ds(16 * j + k, 1), :], (8, 128)) for k in range(KCOL)]
        o_imag = [jnp.broadcast_to(rows[pl.ds(16 * j + 8 + k, 1), :], (8, 128)) for k in range(KCOL)]
        last = n == TERMS - 1

        def body(x2, carry):
            for i in range(2):
                x = x2 * 2 + i
                out = []
                for r in range(tiles):
                    along = jnp.zeros((8, 128), jnp.float32)
                    across = jnp.zeros((8, 128), jnp.float32)
                    for k in range(KCOL):
                        column = columns[k, x, pl.ds(8 * r, 8), :]
                        along = along + column * o_real[k]
                        across = across + column * o_imag[k]
                    total = stage[j, x, pl.ds(8 * r, 8), :] - along - times_i(across, even)
                    out.append(factor * total)
                if not last:
                    for r in range(tiles):
                        tb[n + 1, j, R + x, pl.ds(TOP + 8 * r, 8), :] = out[r]
                    pack(n + 1, j, x2, i, (out[0], out[1][0:4]), (out[3][4:8], out[4]))
                else:
                    for r in range(tiles):
                        result[j, x, pl.ds(8 * r, 8), :] = result[j, x, pl.ds(8 * r, 8), :] + out[r]
            return carry
        lax.fori_loop(part * (width_x // 2 // HALVES), (part + 1) * (width_x // 2 // HALVES), body, 0)

    def combine(j):
        def body(x, carry):
            for r in range(tiles):
                t = [tb[m, j, R + x, pl.ds(TOP + 8 * r, 8), :] for m in range(TERMS)]
                result[j, x, pl.ds(8 * r, 8), :] = (t[0] - t[2]) - times_i(t[1] - t[3], even)
            return carry
        lax.fori_loop(0, width_x, body, 0)

    offset = lax.rem(lax.broadcasted_iota(jnp.int32, (128, 128), 0) - lax.broadcasted_iota(jnp.int32, (128, 128), 1) + 128, 128)
    high = jnp.zeros((128, 128), jnp.float32)
    low = jnp.zeros((128, 128), jnp.float32)
    for k in range(1, R + 1):
        value = np.float32(-0.5 * coefficients[k])
        first = np.float32(value.astype(jnp.bfloat16))
        here = (offset == k) | (offset == 128 - k)
        high = jnp.where(here, first, high)
        low = jnp.where(here, np.float32(value - first), low)
    for side in range(2):
        circle[pl.ds(128 * side, 128), 0:128] = high.astype(jnp.bfloat16)
        circle[pl.ds(128 * side, 128), 128:256] = low.astype(jnp.bfloat16)

    for j in range(ORBS):
        loads[j].wait()

        def first(x2, carry):
            for i in range(2):
                t = [tb[0, j, R + x2 * 2 + i, pl.ds(TOP + 8 * r, 8), :] for r in (0, 1, 3, 4)]
                pack(0, j, x2, i, (t[0], t[1][0:4]), (t[2][4:8], t[3]))
            return carry
        lax.fori_loop(0, width_x // 2, first, 0)
    loads[2].wait()
    loads[3].wait()
    start = []
    for j in range(ORBS):
        start = start + dots(tb.at[0], j, R, TOP, 0, width_x)
    start = pack_line(start)
    pl.semaphore_wait(barrier, len(gx_peers) + len(gy_peers))
    for j in range(ORBS):
        for part in range(HALVES):
            send(y_copy, 0, j, part)
        send(x_copy, 0, j)
        if j == 0:
            reduce_start(0, 0, start)
    loads[4].wait()

    def spread(x, carry):
        plane = pot1[x] + (-1.5 * coefficients[0])
        for part in range(2):
            pot[x, pl.ds(part, width_y, stride=2), :] = plane
        for r in range(tiles):
            here = basis.at[x, pl.ds(4 * r, 4)].reshape(64, 128)
            for k in range(KCOL):
                columns[k, x, pl.ds(8 * r, 8), :] = here[pl.ds(k, 8, stride=8), :]
        return carry

    for n in range(TERMS):
        reduce_start(n, 1, reduce_end(n, 0))
        if n == 0:
            lax.fori_loop(0, width_x, spread, 0)
        for j in range(ORBS):
            along_z(n, j)
        for j in range(ORBS):
            receive_x(n, j)
            along_x(n, j)
            for part in range(HALVES):
                receive_y(n, j, part)
                along_y(n, j, part)
        if n == TERMS - 1:
            for j in range(ORBS):
                combine(j)
        line = reduce_end(n, 1)
        unpack_line(line)
        for j in range(ORBS):
            for part in range(HALVES):
                correct(n, j, part)
                if n < TERMS - 1:
                    send(y_copy, n + 1, j, part)
                    send(x_copy, n + 1, j, sides=(part,))
        if n < TERMS - 1:
            start = []
            for j in range(ORBS):
                start = start + dots(tb.at[n + 1], j, R, TOP, 0, width_x)
            reduce_start(n + 1, 0, pack_line(start))
    for copy in pending:
        copy.wait_send()
    for n in range(TERMS):
        reduce_wait(n, 0, a_ssem)
        reduce_wait(n, 1, b_ssem)


def solution(mesh):
    ngx, ngy = mesh.shape["gx"], mesh.shape["gy"]
    dma = pltpu.SemaphoreType.DMA
    f32, bf16 = jnp.float32, jnp.bfloat16

    def per_device(psi, basis, potential):
        width_x, width_y, depth = potential.shape
        ncell = width_x * ngx * width_y * ngy * depth
        far = pl.BlockSpec(memory_space=pltpu.HBM)
        psi = psi.transpose(0, 2, 3, 1, 4).reshape(ORBS, width_x, 2 * width_y, depth)
        basis = basis.transpose(0, 2, 3, 1, 4)
        out = pl.pallas_call(
            functools.partial(kernel, (ngx, ngy, ncell)),
            out_shape=pltpu.VMEM(psi.shape, f32),
            in_specs=[far] * 3,
            out_specs=pl.BlockSpec(memory_space=pltpu.VMEM),
            scratch_shapes=[
                pltpu.VMEM((TERMS, ORBS, width_x + 2 * R, 72, depth), f32),
                pltpu.VMEM((width_x, width_y, 2, KCOL, depth), f32),
                pltpu.VMEM((KCOL, width_x, 2 * width_y, depth), f32),
                pltpu.VMEM((width_x, width_y, depth), f32),
                pltpu.VMEM((width_x, 2 * width_y, depth), f32),
                pltpu.VMEM(psi.shape, f32),
                pltpu.VMEM((2 * width_x * width_y, 2 * depth), bf16),
                pltpu.VMEM((2 * depth, 2 * depth), bf16),
                pltpu.VMEM((TERMS, ORBS, 2, EDGE * width_x, depth), f32),
                pltpu.VMEM((TERMS, ORBS, 2, EDGE * width_x, depth), f32),
                pltpu.VMEM((32, depth), f32),
                pltpu.VMEM((TERMS, 2, 1, depth), f32),
                pltpu.VMEM((TERMS, 2, 63, 1, depth), f32),
                dma((5,)),
                dma((TERMS, ORBS, 2)),
                dma((TERMS, ORBS, 2)),
                dma((TERMS, ORBS, 2, HALVES)),
                dma((TERMS, ORBS, 2, HALVES)),
                dma((TERMS,)),
                dma((TERMS,)),
                dma((TERMS,)),
                dma((TERMS,)),
            ],
            compiler_params=pltpu.CompilerParams(
                collective_id=0, has_side_effects=True, vmem_limit_bytes=60 * 2**20),
            name="taylor",
        )(psi, basis, potential)
        return out.reshape(ORBS, width_x, width_y, 2, depth).transpose(0, 3, 1, 2, 4)

    placed = (P(None, None, "gx", "gy", None), P(None, None, "gx", "gy", None), P("gx", "gy", None))
    return jax.shard_map(per_device, mesh=mesh, in_specs=placed, out_specs=P(None, None, "gx", "gy", None),
                         check_vma=False)
```

```python
import functools

import jax
import jax.numpy as jnp
import numpy as np
from jax import lax
from jax.experimental import pallas as pl
from jax.experimental.pallas import tpu as pltpu
from jax.sharding import PartitionSpec as P

MESH = pl.DeviceIdType.MESH
coefficients = [
    -5369.0 / 1800.0,
    12.0 / 7.0,
    -15.0 / 56.0,
    10.0 / 189.0,
    -1.0 / 112.0,
    2.0 / 1925.0,
    -1.0 / 16632.0,
]
step_size = 0.25
TERMS = 4
ORBS = 2
KCOL = 8
R = 6
EDGE = 2 * R
HALVES = 2
TOP = 16
GROUP = 4


def times_i(tile, even):
    return jnp.where(even, -pltpu.roll(tile, 7, 0), pltpu.roll(tile, 1, 0))


def kernel(sizes, psi_hbm, basis_hbm, pot_hbm, result, tb, basis, columns, pot1, pot, stage, split, circle, ysend, yrecv, rows, msg, sums,
           load_sem, x_ssem, x_rsem, y_ssem, y_rsem, a_ssem, a_rsem, b_ssem, b_rsem):
    ngx, ngy, ncell = sizes
    width_x, width_r = psi_hbm.shape[1], psi_hbm.shape[2]
    width_y = width_r // 2
    tiles = width_r // 8
    gx, gy = lax.axis_index("gx"), lax.axis_index("gy")
    x_near = [(lax.rem(gx + d, ngx), gy) for d in (ngx - 1, 1)]
    y_near = [(gx, lax.rem(gy + d, ngy)) for d in (ngy - 1, 1)]
    core, chip = lax.rem(gx, 2), gx // 2
    cy, cz = gy // 4, lax.rem(gy, 4)
    x_peers = [(chip * 2 + 1 - core, gy)]
    steps = sorted(((i, j, k) for i in range(4) for j in range(4) for k in range(4) if i + j + k > 0),
                   key=lambda step: -sum(min(d, 4 - d) for d in step))
    y_peers = [(lax.rem(chip + i, 4) * 2 + core, lax.rem(cy + j, 4) * 4 + lax.rem(cz + k, 4)) for i, j, k in steps]
    gx_peers = [(lax.rem(gx + i, ngx), gy) for i in range(1, ngx)]
    gy_peers = [(gx, lax.rem(gy + i, ngy)) for i in sorted(range(1, ngy), key=lambda i: -min(i % 4, 4 - i % 4) - min(i // 4, 4 - i // 4))]

    def peers_of(n, phase):
        return (gx_peers, gy_peers)[phase] if n == 0 else (x_peers, y_peers)[phase]

    inner = pl.ds(TOP, width_r)
    sublane = lax.broadcasted_iota(jnp.int32, (8, 128), 0)
    lane = lax.broadcasted_iota(jnp.int32, (8, 128), 1)
    even = lax.rem(sublane, 2) == 0

    loads = []
    for j in range(ORBS):
        loads.append(pltpu.make_async_copy(psi_hbm.at[j], tb.at[0, j, pl.ds(R, width_x), inner], load_sem.at[j]))
    for part in range(2):
        loads.append(pltpu.make_async_copy(basis_hbm.at[part], basis.at[:, :, part], load_sem.at[2 + part]))
    loads.append(pltpu.make_async_copy(pot_hbm, pot1, load_sem.at[4]))
    for copy in loads:
        copy.start()
    barrier = pltpu.get_barrier_semaphore()
    for peer in gx_peers + gy_peers:
        pl.semaphore_signal(barrier, inc=1, device_id=peer, device_id_type=MESH)

    pending = []

    def pack(n, j, x2, i, low, high):
        base = pl.multiple_of(x2 * 2 * EDGE, 8)
        for side, (first, second) in ((0, low), (1, high)):
            part = ysend.at[n, j, side, pl.ds(base, 2 * EDGE)]
            part[pl.ds(i * EDGE, first.shape[0]), :] = first
            part[pl.ds(i * EDGE + first.shape[0], second.shape[0]), :] = second

    def x_copy(n, j, side):
        src = R if side == 0 else width_x
        dst = width_x + R if side == 0 else 0
        return pltpu.make_async_remote_copy(
            src_ref=tb.at[n, j, pl.ds(src, R), inner], dst_ref=tb.at[n, j, pl.ds(dst, R), inner],
            send_sem=x_ssem.at[n, j, side], recv_sem=x_rsem.at[n, j, 1 - side],
            device_id=x_near[side], device_id_type=MESH)

    def y_copy(n, j, side, part):
        depth = EDGE * width_x // HALVES
        at = pl.ds(part * depth, depth)
        return pltpu.make_async_remote_copy(
            src_ref=ysend.at[n, j, side, at], dst_ref=yrecv.at[n, j, 1 - side, at],
            send_sem=y_ssem.at[n, j, side, part], recv_sem=y_rsem.at[n, j, 1 - side, part],
            device_id=y_near[side], device_id_type=MESH)

    def send(make, *key, sides=(0, 1)):
        for side in sides:
            copy = make(key[0], key[1], side, *key[2:])
            copy.start()
            pending.append(copy)

    def receive_x(n, j):
        for side in range(2):
            x_copy(n, j, side).wait_recv()

    def receive_y(n, j, part):
        for side in range(2):
            y_copy(n, j, side, part).wait_recv()

        def unpack(x2, carry):
            base = pl.multiple_of(x2 * 2 * EDGE, 8)
            for side in range(2):
                rim = yrecv.at[n, j, side, pl.ds(base, 2 * EDGE)]
                at = TOP - EDGE if side == 0 else TOP + width_r
                for i in range(2):
                    tb[n, j, R + x2 * 2 + i, pl.ds(at, EDGE), :] = rim[pl.ds(i * EDGE, EDGE), :]
            return carry
        lax.fori_loop(part * (width_x // 2 // HALVES), (part + 1) * (width_x // 2 // HALVES), unpack, 0)

    def along_z(n, j):
        def halves(x2, carry):
            planes = tb[n, j, pl.ds(R + x2 * 2, 2), inner].reshape(2 * width_r, 128)
            high = planes.astype(jnp.bfloat16)
            at = pl.ds(pl.multiple_of(x2 * 2 * width_r, 16), 2 * width_r)
            split[at, 0:128] = high
            split[at, 128:256] = (planes - high.astype(jnp.float32)).astype(jnp.bfloat16)
            return carry
        lax.fori_loop(0, width_x // 2, halves, 0)
        found = jnp.dot(split[...], circle[...], preferred_element_type=jnp.float32)
        stage[j] = (found[:, 0:128] + found[:, 128:256]).reshape(width_x, width_r, 128)

    half = [-0.5 * c for c in coefficients]

    def along_x(n, j):
        def body(group, carry):
            x0 = group * GROUP
            for r in range(tiles):
                window = [tb[n, j, x0 + i, pl.ds(TOP + 8 * r, 8), :] for i in range(GROUP + 2 * R)]
                for i in range(GROUP):
                    x = x0 + i
                    total = stage[j, x, pl.ds(8 * r, 8), :] + pot[x, pl.ds(8 * r, 8), :] * window[R + i]
                    for k in range(1, R + 1):
                        total = total + half[k] * (window[R + i + k] + window[R + i - k])
                    stage[j, x, pl.ds(8 * r, 8), :] = total
            return carry
        lax.fori_loop(0, width_x // GROUP, body, 0)

    def along_y(n, j, part):
        def body(x, carry):
            for r in range(tiles):
                total = stage[j, x, pl.ds(8 * r, 8), :]
                for k in range(1, R + 1):
                    near = tb[n, j, R + x, pl.ds(TOP + 8 * r + 2 * k, 8), :]
                    near = near + tb[n, j, R + x, pl.ds(TOP + 8 * r - 2 * k, 8), :]
                    total = total + half[k] * near
                stage[j, x, pl.ds(8 * r, 8), :] = total
            return carry
        lax.fori_loop(part * (width_x // HALVES), (part + 1) * (width_x // HALVES), body, 0, unroll=2)

    def dots(field, j, first_x, first_row, low, high):
        def body(x, carry):
            out = list(carry)
            for y in range(width_y):
                br, bi = basis[x, y, 0], basis[x, y, 1]
                real = field[j, first_x + x, pl.ds(first_row + 2 * y, 1), :]
                imag = field[j, first_x + x, pl.ds(first_row + 2 * y + 1, 1), :]
                at = 2 * (y % 2)
                out[at] = out[at] + (br * real + bi * imag)
                out[at + 1] = out[at + 1] + (br * imag - bi * real)
            return tuple(out)
        zero = jnp.zeros((8, 128), jnp.float32)
        found = lax.fori_loop(low, high, body, (zero,) * 4)
        return [(found[i] + found[2 + i]) * (1.0 / ncell) for i in range(2)]

    def pack_line(vectors):
        packed = jnp.zeros((8, 128), jnp.float32)
        for v, vector in enumerate(vectors):
            packed = jnp.where(lane == 8 * v + sublane, jnp.sum(vector, axis=1, keepdims=True), packed)
        return jnp.sum(packed, axis=0, keepdims=True)

    def reduce_start(n, phase, line):
        ssem, rsem = ((a_ssem, a_rsem), (b_ssem, b_rsem))[phase]
        msg[n, phase] = line
        for i, peer in enumerate(peers_of(n, phase)):
            pltpu.make_async_remote_copy(
                src_ref=msg.at[n, phase], dst_ref=sums.at[n, phase, i], send_sem=ssem.at[n], recv_sem=rsem.at[n],
                device_id=peer, device_id_type=MESH).start()

    def reduce_wait(n, phase, sem):
        count = len(peers_of(n, phase))
        every = sums.at[n, phase, pl.ds(0, count)]
        pltpu.make_async_copy(every, every, sem.at[n]).wait()
        return count

    def reduce_end(n, phase):
        count = reduce_wait(n, phase, (a_rsem, b_rsem)[phase])
        parts = [msg[n, phase]] + [sums[n, phase, i] for i in range(count)]
        while len(parts) > 1:
            parts = [sum(parts[i:i + 2][1:], parts[i]) for i in range(0, len(parts), 2)]
        return parts[0]

    def unpack_line(line):
        whole = jnp.broadcast_to(line, (8, 128))
        for v in range(4):
            own = jnp.where(lane == 8 * v + sublane, whole, 0.0)
            rows[pl.ds(8 * v, 8), :] = jnp.broadcast_to(jnp.sum(own, axis=1, keepdims=True), (8, 128))

    def correct(n, j, part):
        factor = step_size / (n + 1)
        o_real = [jnp.broadcast_to(rows[pl.ds(16 * j + k, 1), :], (8, 128)) for k in range(KCOL)]
        o_imag = [jnp.broadcast_to(rows[pl.ds(16 * j + 8 + k, 1), :], (8, 128)) for k in range(KCOL)]
        last = n == TERMS - 1

        def body(x2, carry):
            for i in range(2):
                x = x2 * 2 + i
                out = []
                for r in range(tiles):
                    along = jnp.zeros((8, 128), jnp.float32)
                    across = jnp.zeros((8, 128), jnp.float32)
                    for k in range(KCOL):
                        column = columns[k, x, pl.ds(8 * r, 8), :]
                        along = along + column * o_real[k]
                        across = across + column * o_imag[k]
                    total = stage[j, x, pl.ds(8 * r, 8), :] - along - times_i(across, even)
                    out.append(factor * total)
                if not last:
                    for r in range(tiles):
                        tb[n + 1, j, R + x, pl.ds(TOP + 8 * r, 8), :] = out[r]
                    pack(n + 1, j, x2, i, (out[0], out[1][0:4]), (out[3][4:8], out[4]))
                else:
                    for r in range(tiles):
                        result[j, x, pl.ds(8 * r, 8), :] = result[j, x, pl.ds(8 * r, 8), :] + out[r]
            return carry
        lax.fori_loop(part * (width_x // 2 // HALVES), (part + 1) * (width_x // 2 // HALVES), body, 0)

    def combine(j):
        def body(x, carry):
            for r in range(tiles):
                t = [tb[m, j, R + x, pl.ds(TOP + 8 * r, 8), :] for m in range(TERMS)]
                result[j, x, pl.ds(8 * r, 8), :] = (t[0] - t[2]) - times_i(t[1] - t[3], even)
            return carry
        lax.fori_loop(0, width_x, body, 0)

    offset = lax.rem(lax.broadcasted_iota(jnp.int32, (128, 128), 0) - lax.broadcasted_iota(jnp.int32, (128, 128), 1) + 128, 128)
    high = jnp.zeros((128, 128), jnp.float32)
    low = jnp.zeros((128, 128), jnp.float32)
    for k in range(1, R + 1):
        value = np.float32(-0.5 * coefficients[k])
        first = np.float32(value.astype(jnp.bfloat16))
        here = (offset == k) | (offset == 128 - k)
        high = jnp.where(here, first, high)
        low = jnp.where(here, np.float32(value - first), low)
    for side in range(2):
        circle[pl.ds(128 * side, 128), 0:128] = high.astype(jnp.bfloat16)
        circle[pl.ds(128 * side, 128), 128:256] = low.astype(jnp.bfloat16)

    for j in range(ORBS):
        loads[j].wait()

        def first(x2, carry):
            for i in range(2):
                t = [tb[0, j, R + x2 * 2 + i, pl.ds(TOP + 8 * r, 8), :] for r in (0, 1, 3, 4)]
                pack(0, j, x2, i, (t[0], t[1][0:4]), (t[2][4:8], t[3]))
            return carry
        lax.fori_loop(0, width_x // 2, first, 0)
    loads[2].wait()
    loads[3].wait()
    start = []
    for j in range(ORBS):
        start = start + dots(tb.at[0], j, R, TOP, 0, width_x)
    start = pack_line(start)
    pl.semaphore_wait(barrier, len(gx_peers) + len(gy_peers))
    for j in range(ORBS):
        for part in range(HALVES):
            send(y_copy, 0, j, part)
        send(x_copy, 0, j)
        if j == 0:
            reduce_start(0, 0, start)
    loads[4].wait()

    def spread(x, carry):
        plane = pot1[x] + (-1.5 * coefficients[0])
        for part in range(2):
            pot[x, pl.ds(part, width_y, stride=2), :] = plane
        for r in range(tiles):
            here = basis.at[x, pl.ds(4 * r, 4)].reshape(64, 128)
            for k in range(KCOL):
                columns[k, x, pl.ds(8 * r, 8), :] = here[pl.ds(k, 8, stride=8), :]
        return carry

    for n in range(TERMS):
        if n > 0:
            along_z(n, 0)
        reduce_start(n, 1, reduce_end(n, 0))
        if n == 0:
            lax.fori_loop(0, width_x, spread, 0)
        for j in range(min(n, 1), ORBS):
            along_z(n, j)
        for j in range(ORBS):
            receive_x(n, j)
            along_x(n, j)
            for part in range(HALVES):
                receive_y(n, j, part)
                along_y(n, j, part)
        if n == TERMS - 1:
            for j in range(ORBS):
                combine(j)
        line = reduce_end(n, 1)
        unpack_line(line)
        for j in range(ORBS):
            for part in range(HALVES):
                correct(n, j, part)
                if n < TERMS - 1:
                    send(y_copy, n + 1, j, part)
                    send(x_copy, n + 1, j, sides=(part,))
        if n < TERMS - 1:
            start = []
            for j in range(ORBS):
                start = start + dots(tb.at[n + 1], j, R, TOP, 0, width_x)
            reduce_start(n + 1, 0, pack_line(start))
    for copy in pending:
        copy.wait_send()
    for n in range(TERMS):
        reduce_wait(n, 0, a_ssem)
        reduce_wait(n, 1, b_ssem)


def solution(mesh):
    ngx, ngy = mesh.shape["gx"], mesh.shape["gy"]
    dma = pltpu.SemaphoreType.DMA
    f32, bf16 = jnp.float32, jnp.bfloat16

    def per_device(psi, basis, potential):
        width_x, width_y, depth = potential.shape
        ncell = width_x * ngx * width_y * ngy * depth
        far = pl.BlockSpec(memory_space=pltpu.HBM)
        psi = psi.transpose(0, 2, 3, 1, 4).reshape(ORBS, width_x, 2 * width_y, depth)
        basis = basis.transpose(0, 2, 3, 1, 4)
        out = pl.pallas_call(
            functools.partial(kernel, (ngx, ngy, ncell)),
            out_shape=pltpu.VMEM(psi.shape, f32),
            in_specs=[far] * 3,
            out_specs=pl.BlockSpec(memory_space=pltpu.VMEM),
            scratch_shapes=[
                pltpu.VMEM((TERMS, ORBS, width_x + 2 * R, 72, depth), f32),
                pltpu.VMEM((width_x, width_y, 2, KCOL, depth), f32),
                pltpu.VMEM((KCOL, width_x, 2 * width_y, depth), f32),
                pltpu.VMEM((width_x, width_y, depth), f32),
                pltpu.VMEM((width_x, 2 * width_y, depth), f32),
                pltpu.VMEM(psi.shape, f32),
                pltpu.VMEM((2 * width_x * width_y, 2 * depth), bf16),
                pltpu.VMEM((2 * depth, 2 * depth), bf16),
                pltpu.VMEM((TERMS, ORBS, 2, EDGE * width_x, depth), f32),
                pltpu.VMEM((TERMS, ORBS, 2, EDGE * width_x, depth), f32),
                pltpu.VMEM((32, depth), f32),
                pltpu.VMEM((TERMS, 2, 1, depth), f32),
                pltpu.VMEM((TERMS, 2, 63, 1, depth), f32),
                dma((5,)),
                dma((TERMS, ORBS, 2)),
                dma((TERMS, ORBS, 2)),
                dma((TERMS, ORBS, 2, HALVES)),
                dma((TERMS, ORBS, 2, HALVES)),
                dma((TERMS,)),
                dma((TERMS,)),
                dma((TERMS,)),
                dma((TERMS,)),
            ],
            compiler_params=pltpu.CompilerParams(
                collective_id=0, has_side_effects=True, vmem_limit_bytes=60 * 2**20),
            name="taylor",
        )(psi, basis, potential)
        return out.reshape(ORBS, width_x, width_y, 2, depth).transpose(0, 3, 1, 2, 4)

    placed = (P(None, None, "gx", "gy", None), P(None, None, "gx", "gy", None), P("gx", "gy", None))
    return jax.shard_map(per_device, mesh=mesh, in_specs=placed, out_specs=P(None, None, "gx", "gy", None),
                         check_vma=False)
```
